32 devices in a mesh: groups: 2 (over y), pool: 4 (over z), tensor: 2 (over x), rep: 2 (over core).
Axes of the slice: x: 2, y: 2, z: 4, core: 2. Of those that a mesh axis runs over, the one named last changes fastest.
Arguments:
- request_slot: int32 [128], P(('groups', 'pool', 'rep')), parts along dimension 0, may hold values from 0 to 63, as said below
- lengths: int32 [128], P(('groups', 'pool', 'rep')), parts along dimension 0, may hold values from 24 to 192, as said below
- prefill_slot: int32 [16], P(('groups', 'pool', 'rep')), parts along dimension 0, may hold values from 0 to 7
- prefill_offset: int32 [16], P(('groups', 'pool', 'rep')), parts along dimension 0, may hold values from 0 to 184
- queries: bfloat16 [128, 3, 8192], P(('groups', 'pool', 'rep'), None, 'tensor'), parts along dimension 0, may hold values from -8 to 8
- new_kv: bfloat16 [128, 3, 2, 1024], P(('groups', 'pool', 'rep'), None, None, 'tensor'), parts along dimension 0, may hold values from -6 to 6
- kv_cache: bfloat16 [128, 192, 2, 1024], P(('groups', 'pool', 'rep'), None, None, 'tensor'), parts along dimension 0, may hold values from -8 to 8
- prefill_kv: bfloat16 [16, 8, 2, 1024], P('groups', ('pool', 'rep'), None, 'tensor'), parts along dimension 0, may hold values from -6 to 6
- out_weight: bfloat16 [8192, 8192], P('tensor', ('pool', 'rep')), may hold values from -0.5 to 0.5
Outputs:
- layer_out: bfloat16 [384, 8192], P(('groups', 'tensor'), ('pool', 'rep')), parts along dimension 0
The draws below stay inside these ranges and needn't reach their ends.
There are 2 independent parts, one for each index of `groups`. The reference program is written for one: setup_inputs(seed, part) draws one part's arguments, and reference() takes and returns one part's arrays. A program takes and returns all parts, laid end to end along the dimension named above; an argument that names none is the same for every part. Nothing has to cross between parts.
Inputs may be any that keep to these rules, and one draw needn't show every extreme that they name: `request_slot`: A permutation of the 64 slots; slot s lies on pool device s // 8. The 8 requests of one device name at most 2 slots of any one pool device, and in every draw some device names 2 slots of one pool device. Every prefill block lies within its request's length: prefill_offset[o] + 8 <= lengths[o * 8 + prefill_slot[o]].
All inputs are finite; a program needn't handle non-finite values.
Results may differ from the reference program's by a relative error of at most 0.0057.
Values may be sent and summed in bfloat16 or wider, within the bound.
A program may use at most 64 MiB of HBM per device.

```python
import jax
import jax.numpy as jnp
from jax import lax

D = 8192
HEADS = 64
KV_HEADS = 8
HEAD_DIM = 128
GROUP = 8
CTX = 192
DRAFT = 3
OWNERS = 8
SLOTS = 8
REQUESTS = 64
ROWS = 192
STRETCH = 8


def context_plan(key):
    subkeys = jax.random.split(jax.random.fold_in(key, 71), 7)
    levels = jax.random.randint(subkeys[0], (OWNERS, 1), 1, 5)
    lowest = levels * CTX // 8
    upper = levels * CTX // 4 + 1
    spans = jax.random.randint(subkeys[1], (OWNERS, SLOTS), lowest, upper)
    longest = jax.random.randint(subkeys[2], (), 0, OWNERS * SLOTS)
    spans = jnp.where(jnp.arange(OWNERS * SLOTS).reshape(OWNERS, SLOTS) == longest, CTX, spans)
    chosen_slot = jax.random.randint(subkeys[3], (OWNERS,), 0, SLOTS)
    starts = jax.random.randint(subkeys[4], (OWNERS,), 0, CTX - STRETCH + 1)
    far_owner = jax.random.randint(subkeys[5], (), 0, OWNERS)
    near_owner = (far_owner + 1 + jax.random.randint(subkeys[6], (), 0, OWNERS - 1)) % OWNERS
    owner_ids = jnp.arange(OWNERS)
    starts = jnp.where(owner_ids == far_owner, CTX - STRETCH, starts)
    starts = jnp.where(owner_ids == near_owner, 0, starts)
    chosen = jnp.arange(SLOTS)[None, :] == chosen_slot[:, None]
    spans = jnp.where(chosen, jnp.maximum(spans, starts[:, None] + STRETCH), spans)
    return (spans.reshape(-1).astype(jnp.int32), chosen_slot.astype(jnp.int32), starts.astype(jnp.int32))


def draw_lengths(key, part):
    spans, chosen_slot, starts = context_plan(key)
    return spans


def draw_prefill_slot(key, part):
    spans, chosen_slot, starts = context_plan(key)
    return chosen_slot


def draw_prefill_offset(key, part):
    spans, chosen_slot, starts = context_plan(key)
    return starts


def draw_request_slot(key, part):
    key = jax.random.fold_in(key, 11)
    subkeys = jax.random.split(key, 5)
    shifts = jax.random.permutation(subkeys[0], OWNERS)
    doubled = jax.random.randint(subkeys[1], (), 1, OWNERS // 2 + 1)
    ordering = jax.random.permutation(subkeys[2], OWNERS)
    series = jnp.arange(OWNERS)
    offsets = jnp.where(series < 2 * doubled, ordering[series // 2], ordering[series])
    shuffles = jax.vmap(lambda one_key: jax.random.permutation(one_key, OWNERS))(jax.random.split(subkeys[3], OWNERS))
    owners_of = (shifts[:, None] + offsets[shuffles]) % OWNERS
    flat_owner = owners_of.reshape(-1)
    linear = jnp.arange(REQUESTS)
    before = (flat_owner[None, :] == flat_owner[:, None]) & (linear[None, :] < linear[:, None])
    rank_within = jnp.sum(before.astype(jnp.int32), axis=1)
    slot_orders = jax.vmap(lambda one_key: jax.random.permutation(one_key, SLOTS))(jax.random.split(subkeys[4], OWNERS))
    local_slot = slot_orders[flat_owner, rank_within]
    return (flat_owner * SLOTS + local_slot).astype(jnp.int32)


def draw_queries(key, part):
    key = jax.random.fold_in(key, 1)
    shape = (REQUESTS, DRAFT, HEADS, HEAD_DIM)
    entries = jnp.clip(jax.random.normal(key, shape, jnp.float32), -8.0, 8.0)
    return entries.reshape(REQUESTS, DRAFT, HEADS * HEAD_DIM).astype(jnp.bfloat16)


def draw_kv_cache(key, part):
    key = jax.random.fold_in(key, 2)
    shape = (REQUESTS, CTX, 2, KV_HEADS * HEAD_DIM)
    entries = jnp.clip(jax.random.normal(key, shape, jnp.float32), -8.0, 8.0)
    return entries.astype(jnp.bfloat16)


def block_scale(key, dims, shards, low, top_value):
    def one(dim, shards_of):
        heights = jax.random.uniform(jax.random.fold_in(jax.random.fold_in(key, 6), dim), (shards_of,), jnp.float32, low / len(shards), top_value / len(shards))
        return jnp.repeat(jnp.exp(heights), dims[dim] // shards_of).reshape((-1,) + (1,) * (len(dims) - dim - 1))

    loudness = one(*shards[0])
    for cut in shards[1:]:
        loudness = loudness * one(*cut)
    return loudness


def gaussian(own_key, extent, width, most, cuts=(), kind=jnp.bfloat16):
    drawn = jax.random.normal(own_key, extent, jnp.float32) * width
    if len(cuts) > 0:
        drawn = block_scale(own_key, extent, cuts, -0.22, 0.18) * drawn
    return jnp.clip(drawn, min=-most, max=most).astype(kind)


def setup_inputs(seed: int = 0, part: int = 0) -> dict:
    key_of = jax.random.split(jax.random.key(seed), 10)
    part_splits = jax.random.split(jax.random.fold_in(key_of[9], part), 10)
    return {
        "request_slot": draw_request_slot(jax.random.fold_in(jax.random.fold_in(key_of[9], part), 71), part),
        "lengths": draw_lengths(jax.random.fold_in(jax.random.fold_in(key_of[9], part), 71), part),
        "prefill_slot": draw_prefill_slot(jax.random.fold_in(jax.random.fold_in(key_of[9], part), 71), part),
        "prefill_offset": draw_prefill_offset(jax.random.fold_in(jax.random.fold_in(key_of[9], part), 71), part),
        "queries": draw_queries(jax.random.fold_in(jax.random.fold_in(key_of[9], part), 71), part),
        "new_kv": gaussian(part_splits[5], (REQUESTS, DRAFT, 2, KV_HEADS * HEAD_DIM), 1.0, 6.0, ((0, 8), (3, 2))),
        "kv_cache": draw_kv_cache(jax.random.fold_in(jax.random.fold_in(key_of[9], part), 71), part),
        "prefill_kv": gaussian(part_splits[7], (OWNERS, STRETCH, 2, KV_HEADS * HEAD_DIM), 1.0, 6.0, ((1, 8), (3, 2))),
        "out_weight": gaussian(key_of[8], (HEADS * HEAD_DIM, D), HEAD_DIM ** -0.5, 0.5, ((0, 2), (1, 8))),
    }


def reference(request_slot, lengths, prefill_slot, prefill_offset, queries, new_kv, kv_cache, prefill_kv, out_weight):
    places = jnp.arange(OWNERS, dtype=jnp.int32) * SLOTS + prefill_slot.astype(jnp.int32)
    positions = prefill_offset.astype(jnp.int32)[:, None] + jnp.arange(STRETCH, dtype=jnp.int32)[None, :]
    cache_full = kv_cache.at[places[:, None], positions].set(prefill_kv)
    score_scale = HEAD_DIM ** -0.5
    causal = jnp.arange(DRAFT)[:, None] >= jnp.arange(DRAFT)[None, :]

    def attend(request):
        slot_index = request_slot[request].astype(jnp.int32)
        length = lengths[slot_index]
        query_rows = queries[request].reshape(DRAFT, KV_HEADS, GROUP, HEAD_DIM).astype(jnp.float32)
        stored = cache_full[slot_index].reshape(CTX, 2, KV_HEADS, HEAD_DIM).astype(jnp.float32)
        fresh_pair = new_kv[request].reshape(DRAFT, 2, KV_HEADS, HEAD_DIM).astype(jnp.float32)
        cached_scores = jnp.einsum("dkgh,tkh->kgdt", query_rows, stored[:, 0]) * score_scale
        new_scores = jnp.einsum("dkgh,ekh->kgde", query_rows, fresh_pair[:, 0]) * score_scale
        visible = jnp.arange(CTX)[None, None, None, :] < length
        cached_scores = jnp.where(visible, cached_scores, -jnp.inf)
        new_scores = jnp.where(causal, new_scores, -jnp.inf)
        highest = jnp.maximum(jnp.max(cached_scores, axis=-1), jnp.max(new_scores, axis=-1))
        cached_exp = jnp.exp(cached_scores - highest[..., None])
        new_exp = jnp.exp(new_scores - highest[..., None])
        denominator = jnp.sum(cached_exp, axis=-1) + jnp.sum(new_exp, axis=-1)
        cached_weight = lax.optimization_barrier((cached_exp / denominator[..., None]).astype(jnp.bfloat16)).astype(jnp.float32)
        new_weight = lax.optimization_barrier((new_exp / denominator[..., None]).astype(jnp.bfloat16)).astype(jnp.float32)
        summed = jnp.einsum("kgdt,tkh->dkgh", cached_weight, stored[:, 1])
        summed = summed + jnp.einsum("kgde,ekh->dkgh", new_weight, fresh_pair[:, 1])
        return summed.astype(jnp.bfloat16).reshape(DRAFT, HEADS * HEAD_DIM)

    attention = lax.map(attend, jnp.arange(REQUESTS, dtype=jnp.int32))
    attention = attention.reshape(ROWS, HEADS * HEAD_DIM)
    return jnp.dot(attention, out_weight, preferred_element_type=jnp.float32).astype(jnp.bfloat16)
```

```python
import functools

import jax
import jax.numpy as jnp
from jax import lax
from jax.experimental import pallas as pl
from jax.experimental.pallas import tpu as pltpu
from jax.sharding import PartitionSpec as P

HD = 128
DRAFT = 3
CAP = 2
KEYS = 64
PACK = 64
F32 = jnp.float32
BF16 = jnp.bfloat16
MESH = pl.DeviceIdType.MESH


def log2(n):
    assert n & (n - 1) == 0
    return n.bit_length() - 1


def up(n, m):
    return (n + m - 1) // m * m


def iota(shape, dim):
    return lax.broadcasted_iota(jnp.int32, shape, dim)


def kernel(dims, slot_s, len_s, pslot_s, poff_s, src, cache, weight, out,
           kvbuf, wbuf, pack, recv, meta_out, meta_in, perm, cmat, gath, ytot, ysend, yrecv,
           kv_sem, w_sem, self_sem, pk_send, pk_recv, mt_send, mt_recv, g_send, g_recv, y_send, y_recv):
    S, O, R, T, K, CTX, GS, N, NT = dims
    PL = O // R
    ls, lo = log2(S), log2(O)
    lg = log2(GS)
    gw = GS * HD
    half = GS // 2
    PR = max(16, O)
    z, core, me_t = lax.axis_index("pool"), lax.axis_index("rep"), lax.axis_index("tensor")
    me = z * R + core
    rows_t = S * O * DRAFT // T

    for k in range(K):
        pltpu.make_async_copy(
            cache.at[:, :, :, pl.ds(k * HD, HD)], kvbuf.at[k], kv_sem.at[k]).start()
    for k in range(K):
        pltpu.make_async_copy(
            weight.at[pl.ds(k * gw, gw), :], wbuf.at[k], w_sem.at[k]).start()

    barrier = pltpu.get_barrier_semaphore()
    for i in range(1, O):
        p = lax.rem(me + i, O)
        pl.semaphore_signal(barrier, inc=1, device_id={"pool": p // R, "rep": lax.rem(p, R)},
                            device_id_type=MESH)
    for i in range(1, T):
        pl.semaphore_signal(barrier, inc=1, device_id={"tensor": lax.rem(me_t + i, T)},
                            device_id_type=MESH)

    slots = [slot_s[r] for r in range(S)]
    orow = iota((O, 128), 0)
    lane = iota((O, 128), 1)
    seen = jnp.zeros((O, 128), jnp.int32)
    note = jnp.zeros((O, 128), jnp.int32)
    for r in range(S):
        hit = orow == (slots[r] >> ls)
        note = jnp.where(hit & (seen == (lane & 1)), (slots[r] & (S - 1)) + 1, note)
        seen = seen + jnp.where(hit, 1, 0)
    MR = meta_out.shape[1]
    L = (iota((MR, 128), 0) - 1) * 128 + iota((MR, 128), 1) - me * (S * DRAFT)
    keyed = jnp.zeros((MR, 128), jnp.int32)
    for r in range(S):
        keyed = jnp.where((L >= DRAFT * r) & (L < DRAFT * r + DRAFT),
                          slots[r] * 4 + 1 - DRAFT * r + L, keyed)
    first = iota((MR, 128), 0) == 0
    for o in range(O):
        meta_out[o] = jnp.where(first, jnp.broadcast_to(note[o:o + 1], (MR, 128)), keyed)

    NQ, NF = S * DRAFT * GS, S * DRAFT * 2
    NC = src.shape[0]
    c = iota((1, NC), 1)
    f = c - NQ
    pre = c - NQ - NF
    is_q = c < NQ
    is_f = (c >= NQ) & (pre < 0)
    rcol = jnp.where(is_q, (c >> lg) & (S - 1), jnp.where(is_f, (f >> 1) & (S - 1), -1))
    ocol = jnp.zeros((1, NC), jnp.int32) - 1
    for r in range(S):
        ocol = jnp.where(rcol == r, slots[r] >> ls, ocol)
    rank = jnp.zeros((1, NC), jnp.int32)
    for r in range(S):
        rank = rank + jnp.where((rcol > r) & (ocol == (slots[r] >> ls)), 1, 0)
    code = (ocol * CAP + rank) * KEYS
    ckey = jnp.where(
        is_q, code + (c >> (lg + ls)) * GS + (c & (GS - 1)),
        jnp.where(is_f, code + 24 + (f >> (1 + ls)) * 2 + (f & 1),
                  (pre >> 1) * CAP * KEYS + 32 + (pre & 1)))
    OB = min(O, 8)
    jr = iota((OB * PACK, 1), 0)
    j = jr & (PACK - 1)
    jf = j - 48
    jkey = jnp.where(j < 48, (j & 1) * KEYS + (j >> 4) * GS + ((j >> 1) & (GS - 1)),
                     jnp.where(j < 60, (j & 1) * KEYS + 24 + (jf >> 2) * 2 + ((jf >> 1) & 1),
                               jnp.where(j < 62, 32 + j - 60, -1000000)))
    jkey = jkey + (jr >> 6) * CAP * KEYS
    for b in range(O // OB):
        place = jnp.where(jkey + b * OB * CAP * KEYS == ckey, 1.0, 0.0).astype(BF16)
        packed = jnp.dot(place, src[...], preferred_element_type=F32).astype(BF16)
        for k in range(K):
            pack[k, b * OB:(b + 1) * OB] = packed[:, k * HD:(k + 1) * HD].reshape(OB, PACK, HD)

    pl.semaphore_wait(barrier, O - 1 + T - 1)

    def peer(i):
        p = lax.rem(me + i, O)
        return p, {"pool": p // R, "rep": lax.rem(p, R)}

    def meta_copy(i):
        p, dev = peer(i)
        return pltpu.make_async_remote_copy(
            meta_out.at[p], meta_in.at[me], mt_send.at[p], mt_recv.at[me], dev, MESH)

    def pack_copy(k, i):
        p, dev = peer(i)
        return pltpu.make_async_remote_copy(
            pack.at[k, p], recv.at[k, me], pk_send.at[k, p], pk_recv.at[k, me], dev, MESH)

    own_copies = [pltpu.make_async_copy(meta_out.at[me], meta_in.at[me], self_sem.at[K])]
    for k in range(K):
        own_copies.append(pltpu.make_async_copy(pack.at[k, me], recv.at[k, me], self_sem.at[k]))
    for cp in own_copies:
        cp.start()
    order = list(range(1, O))
    for i in order:
        meta_copy(i).start()
    for k in range(K):
        for i in order:
            pack_copy(k, i).start()

    def wait_arrival(buf, sem):
        pltpu.make_async_copy(buf, buf, sem).wait()

    own_copies[0].wait()
    for i in order:
        p, _ = peer(i)
        wait_arrival(meta_in.at[p], mt_recv.at[p])

    def row_keys():
        q = iota((NQ, 1), 0)
        qk = (((q >> lg) & (S - 1)) + 1) * KEYS + (q >> (lg + ls)) * GS + (q & (GS - 1))
        fr = iota((S * 16, 1), 0)
        e = fr & 15
        pr = iota((PR, 1), 0)
        parts = [qk]
        for kv in range(2):
            parts.append(jnp.where(e < DRAFT, ((fr >> 4) + 1) * KEYS + 24 + e * 2 + kv, -2))
            parts.append(jnp.where(pr < O, (S + 2) * KEYS + pr * 2 + kv, -2))
        return parts

    parts = row_keys()
    l128 = iota((1, 128), 1)
    jl = l128 & (PACK - 1)
    jlf = jl - 48
    stat = jnp.where(jl < 48, (jl >> 4) * GS + ((jl >> 1) & (GS - 1)),
                     24 + (jlf >> 2) * 2 + ((jlf >> 1) & 1))
    for pair in range(O // 2):
        m = jnp.where(l128 < PACK, meta_in[2 * pair, 0:1, :], meta_in[2 * pair + 1, 0:1, :])
        srcidx = 2 * pair + (l128 >> 6)
        key = jnp.where(jl < 60, m * KEYS + stat,
                        jnp.where(jl < 62, (S + 2) * KEYS + srcidx * 2 + jl - 60, -1))
        row = 0
        for part in parts:
            n = part.shape[0]
            perm[row:row + n, pair * 128:(pair + 1) * 128] = jnp.where(part == key, 1.0, 0.0).astype(BF16)
            row += n

    def out_onehots(keys):
        g = iota((O * 2 * S, 1), 0)
        hi = (g >> ls) & 1
        slot4 = (((g >> (ls + 1)) << ls) + (g & (S - 1))) * 4 + 1
        res = []
        for kk in (slot4 + hi, jnp.where(hi == 0, slot4 + 2, -1), jnp.where(hi == 1, slot4 + 2, -1)):
            res.append(jnp.transpose(jnp.where(kk == keys, 1.0, 0.0)).astype(BF16))
        return res

    total = meta_in[0]
    for o in range(1, O):
        total = total + meta_in[o]
    keep = cmat is not None
    if keep:
        for t in range(NT):
            for x, m in enumerate(out_onehots(total[1 + t:2 + t])):
                cmat[x, t * 128:(t + 1) * 128, :] = m
    else:
        for i in order:
            meta_copy(i).wait_send()
        meta_out[0] = total

    pslot, poff = pslot_s[0], poff_s[0]
    jc = iota((1, 2 * CTX), 1)
    tc = jc >> 1
    neg = jnp.float32(-jnp.inf)
    lp = iota((1, PR + 16), 1)
    drow = iota((DRAFT * GS, PR + 16), 0) >> lg
    lane_e = iota((DRAFT * GS, PR + 16), 1)
    fresh_ok = (lane_e >= PR) & (lane_e - PR <= drow)
    scale = HD ** -0.5
    si = iota((S * GS, S * GS), 0)
    sj = iota((S * GS, S * GS), 1)
    swap = jnp.where(((si & (S - 1)) == (sj >> lg)) & ((si >> ls) == (sj & (GS - 1))), 1.0, 0.0).astype(BF16)

    def attend(k):
        took = jnp.dot(perm[...], recv[k].reshape(O * PACK, HD), preferred_element_type=F32)
        fk0 = NQ
        pk0 = fk0 + S * 16
        fv0 = pk0 + PR
        pv0 = fv0 + S * 16
        pre_k, pre_v = took[pk0:pk0 + PR].astype(BF16), took[pv0:pv0 + PR].astype(BF16)
        sc, se, xs, vs = [], [], [], []
        for s in range(S):
            q = jnp.concatenate([took[(d * S + s) * GS:(d * S + s + 1) * GS] for d in range(DRAFT)], 0).astype(BF16)
            x = kvbuf[k, s].reshape(2 * CTX, HD)
            ek = jnp.concatenate([pre_k, took[fk0 + s * 16:fk0 + s * 16 + 16].astype(BF16)], 0)
            ev = jnp.concatenate([pre_v, took[fv0 + s * 16:fv0 + s * 16 + 16].astype(BF16)], 0)
            nt = (((1,), (1,)), ((), ()))
            a = lax.dot_general(q, x, nt, preferred_element_type=F32) * scale
            b = lax.dot_general(q, ek, nt, preferred_element_type=F32) * scale
            mine = s == pslot
            lo_t = jnp.where(mine, poff, CTX)
            ok = ((jc & 1) == 0) & (tc < len_s[s]) & ((tc < lo_t) | (tc >= lo_t + O))
            pre_lim = jnp.where(mine, O, 0)
            sc.append(jnp.where(ok, a, neg))
            se.append(jnp.where(fresh_ok | (lane_e < pre_lim), b, neg))
            xs.append(x)
            vs.append(ev)
        outs = []
        for s in range(S):
            top = jnp.maximum(jnp.max(sc[s], axis=1, keepdims=True), jnp.max(se[s], axis=1, keepdims=True))
            pa, pb = jnp.exp(sc[s] - top), jnp.exp(se[s] - top)
            inv = 1.0 / (jnp.sum(pa, axis=1, keepdims=True) + jnp.sum(pb, axis=1, keepdims=True))
            wa = pltpu.roll(pa * inv, 1, 1).astype(BF16)
            wb = (pb * inv).astype(BF16)
            outs.append(jnp.dot(wa, xs[s], preferred_element_type=F32)
                        + jnp.dot(wb, vs[s], preferred_element_type=F32))
        turned = []
        for d in range(DRAFT):
            rows = jnp.concatenate([o[d * GS:(d + 1) * GS] for o in outs], 0).astype(BF16)
            turned.append(jnp.dot(swap, rows, preferred_element_type=F32))
        for g in range(GS):
            gath[k, me, :, g * HD:(g + 1) * HD] = jnp.concatenate(
                [turned[0][g * S:(g + 1) * S], turned[1][g * S:(g + 1) * S]], 0).astype(BF16)
        for g in range(half):
            gath[k, me, :, gw + g * HD:gw + (g + 1) * HD] = jnp.concatenate(
                [turned[2][g * S:(g + 1) * S], turned[2][(g + half) * S:(g + half + 1) * S]], 0).astype(BF16)

    def g_copy(k, block, way):
        dev = [{"pool": z + 1}, {"pool": z - 1}, {"rep": 1 - core}][way]
        ref = gath.at[k, block]
        return pltpu.make_async_remote_copy(ref, ref, g_send.at[k, block, way], g_recv.at[k, block], dev, MESH)

    sends = []

    def g_start(k, cond, block, way):
        sends.append((k, cond, block, way))

        @pl.when(cond)
        def _():
            g_copy(k, block, way).start()

    always = z >= 0

    def hop(k, h):
        if h == 0:
            g_start(k, z < PL - 1, me, 0)
            g_start(k, z > 0, me, 1)
            g_start(k, always, me, 2)
            return
        for way, zz in ((0, z - h), (1, z + h)):
            there = (zz >= 0) & (zz < PL)
            block = jnp.clip(zz, 0, PL - 1) * R + core

            @pl.when(there)
            def _():
                wait_arrival(gath.at[k, block], g_recv.at[k, block])

            g_start(k, there & ((z < PL - 1) if way == 0 else (z > 0)), block, way)
            g_start(k, there, block, 2)

    def other_core(k):
        for zz in range(PL):
            block = zz * R + 1 - core
            wait_arrival(gath.at[k, block], g_recv.at[k, block])

    def picked(k, mats):
        g = gath[k].reshape(O * 2 * S, gw + gw // 2)
        a = jnp.dot(mats[0], g[:, :gw], preferred_element_type=F32)
        b = jnp.dot(mats[1], g[:, gw:], preferred_element_type=F32)
        c2 = jnp.dot(mats[2], g[:, gw:], preferred_element_type=F32)
        return (a + jnp.concatenate([b, c2], 1)).astype(BF16)

    def y_copy(n, i):
        p = lax.rem(me_t + i, T)
        return pltpu.make_async_remote_copy(
            ysend.at[n, p], yrecv.at[n, me_t], y_send.at[n, p], y_recv.at[n, me_t], {"tensor": p}, MESH)

    NCH = ysend.shape[0]
    cw = N // NCH

    def share(n):
        for t in range(T):
            ysend[n, t] = ytot[t * rows_t:(t + 1) * rows_t, n * cw:(n + 1) * cw].astype(BF16)
        for i in range(1, T):
            y_copy(n, i).start()

    def project(k):
        pltpu.make_async_copy(weight.at[pl.ds(k * gw, gw), :], wbuf.at[k], w_sem.at[k]).wait()
        if keep:
            rows = picked(k, [cmat[x] for x in range(3)])
            for n in range(NCH):
                cols = slice(n * cw, (n + 1) * cw)
                y = jnp.dot(rows, wbuf[k, :, cols], preferred_element_type=F32)
                ytot[:, cols] = y if k == 0 else ytot[:, cols] + y
                if k == K - 1:
                    share(n)
        else:
            def body(t, carry):
                rows = picked(k, out_onehots(meta_out[0, pl.ds(1 + t, 1), :]))
                at = pl.ds(pl.multiple_of(t * 128, 128), 128)
                y = jnp.dot(rows, wbuf[k], preferred_element_type=F32)
                ytot[at, :] = y if k == 0 else ytot[at, :] + y
                return carry

            lax.fori_loop(0, NT, body, 0)
            if k == K - 1:
                for n in range(NCH):
                    share(n)

    for step in range(K + PL):
        if step < K:
            k = step
            pltpu.make_async_copy(cache.at[:, :, :, pl.ds(k * HD, HD)], kvbuf.at[k], kv_sem.at[k]).wait()
            own_copies[1 + k].wait()
            for i in order:
                p, _ = peer(i)
                wait_arrival(recv.at[k, p], pk_recv.at[k, p])
            attend(k)
            hop(k, 0)
        for h in range(1, PL):
            if 0 <= step - h < K:
                hop(step - h, h)
        k = step - PL
        if 0 <= k < K:
            other_core(k)
            project(k)

    for n in range(NCH):
        cols = slice(n * cw, (n + 1) * cw)
        y = ytot[pl.ds(pl.multiple_of(me_t * rows_t, 32), rows_t), cols]
        for i in range(1, T):
            p = lax.rem(me_t + i, T)
            wait_arrival(yrecv.at[n, p], y_recv.at[n, p])
            y = y + yrecv[n, p].astype(F32)
        out[:, cols] = y.astype(BF16)

    if keep:
        for i in order:
            meta_copy(i).wait_send()
    for k in range(K):
        for i in order:
            pack_copy(k, i).wait_send()
    for k, cond, block, way in sends:
        @pl.when(cond)
        def _():
            g_copy(k, block, way).wait_send()
    for n in range(NCH):
        for i in range(1, T):
            y_copy(n, i).wait_send()


def on_device(request_slot, lengths, prefill_slot, prefill_offset, queries, new_kv, kv_cache,
              prefill_kv, out_weight):
    PLn, R, T = lax.axis_size("pool"), lax.axis_size("rep"), lax.axis_size("tensor")
    O = PLn * R
    S = lengths.shape[0]
    CTX = kv_cache.shape[1]
    K = kv_cache.shape[3] // HD
    GS = queries.shape[2] // kv_cache.shape[3]
    N = out_weight.shape[1]
    rows = O * S * DRAFT
    NT = up(rows, 128) // 128
    gw = GS * HD
    src = jnp.concatenate([
        queries.reshape(S, DRAFT, K, GS, HD).transpose(1, 0, 3, 2, 4).reshape(-1, K * HD),
        new_kv.transpose(1, 0, 2, 3).reshape(-1, K * HD),
        prefill_kv.reshape(-1, K * HD),
    ], 0)
    PR = max(16, O)
    MR = up(1 + NT, 8)
    perm_rows = S * DRAFT * GS + 2 * (S * 16 + PR)
    keep = NT <= 2
    NCH = 4
    dims = (S, O, R, T, K, CTX, GS, N, NT)
    scratch = [
        pltpu.VMEM((K, S, CTX, 2, HD), BF16),
        pltpu.VMEM((K, gw, N), BF16),
        pltpu.VMEM((K, O, PACK, HD), BF16),
        pltpu.VMEM((K, O, PACK, HD), BF16),
        pltpu.VMEM((O, MR, 128), jnp.int32),
        pltpu.VMEM((O, MR, 128), jnp.int32),
        pltpu.VMEM((perm_rows, O * PACK), BF16),
    ]
    if keep:
        scratch.append(pltpu.VMEM((3, NT * 128, O * 2 * S), BF16))
    scratch += [
        pltpu.VMEM((K, O, 2 * S, gw + gw // 2), BF16),
        pltpu.VMEM((NT * 128, N), F32),
        pltpu.VMEM((NCH, T, rows // T, N // NCH), BF16),
        pltpu.VMEM((NCH, T, rows // T, N // NCH), BF16),
    ]
    D = pltpu.SemaphoreType.DMA
    scratch += [D((K,)), D((K,)), D((K + 1,)), D((K, O)), D((K, O)), D((O,)), D((O,)),
                D((K, O, 3)), D((K, O)), D((NCH, T)), D((NCH, T))]
    if keep:
        body = functools.partial(kernel, dims)
    else:
        def body(*refs):
            return kernel(dims, *refs[:15], None, *refs[15:])
    smem = pl.BlockSpec(memory_space=pltpu.SMEM)
    vmem = pl.BlockSpec(memory_space=pltpu.VMEM)
    hbm = pl.BlockSpec(memory_space=pl.ANY)
    return pl.pallas_call(
        body,
        out_shape=jax.ShapeDtypeStruct((rows // T, N), BF16),
        in_specs=[smem] * 4 + [vmem, hbm, hbm],
        out_specs=vmem,
        scratch_shapes=scratch,
        compiler_params=pltpu.CompilerParams(
            collective_id=0, has_side_effects=True, vmem_limit_bytes=56 * 1024 * 1024),
        cost_estimate=pl.CostEstimate(flops=4 * 10 ** 9, bytes_accessed=12 * 10 ** 6, transcendentals=10 ** 6),
    )(request_slot, lengths, prefill_slot, prefill_offset, src, kv_cache, out_weight)


def solution(mesh):
    owner = ("groups", "pool", "rep")
    return jax.shard_map(
        on_device,
        mesh=mesh,
        in_specs=(
            P(owner), P(owner), P(owner), P(owner),
            P(owner, None, "tensor"),
            P(owner, None, None, "tensor"),
            P(owner, None, None, "tensor"),
            P("groups", ("pool", "rep"), None, "tensor"),
            P("tensor", ("pool", "rep")),
        ),
        out_specs=P(("groups", "tensor"), ("pool", "rep")),
        check_vma=False,
    )
```

```python
import functools

import jax
import jax.numpy as jnp
from jax import lax
from jax.experimental import pallas as pl
from jax.experimental.pallas import tpu as pltpu
from jax.sharding import PartitionSpec as P

HD = 128
DRAFT = 3
CAP = 2
KEYS = 64
PACK = 64
F32 = jnp.float32
BF16 = jnp.bfloat16
MESH = pl.DeviceIdType.MESH


def log2(n):
    assert n & (n - 1) == 0
    return n.bit_length() - 1


def up(n, m):
    return (n + m - 1) // m * m


def iota(shape, dim):
    return lax.broadcasted_iota(jnp.int32, shape, dim)


def kernel(dims, slot_s, len_s, pslot_s, poff_s, src, cache, weight, out,
           kvbuf, wbuf, pack, recv, meta_out, meta_in, perm, cmat, gath, ytot, ysend, yrecv,
           kv_sem, w_sem, self_sem, pk_send, pk_recv, mt_send, mt_recv, g_send, g_recv, y_send, y_recv):
    S, O, R, T, K, CTX, GS, N, NT = dims
    PL = O // R
    ls, lo = log2(S), log2(O)
    lg = log2(GS)
    gw = GS * HD
    half = GS // 2
    PR = max(16, O)
    z, core, me_t = lax.axis_index("pool"), lax.axis_index("rep"), lax.axis_index("tensor")
    me = z * R + core
    rows_t = S * O * DRAFT // T

    for k in range(K):
        pltpu.make_async_copy(
            cache.at[:, :, :, pl.ds(k * HD, HD)], kvbuf.at[k], kv_sem.at[k]).start()

    barrier = pltpu.get_barrier_semaphore()
    for i in range(1, O):
        p = lax.rem(me + i, O)
        pl.semaphore_signal(barrier, inc=1, device_id={"pool": p // R, "rep": lax.rem(p, R)},
                            device_id_type=MESH)
    for i in range(1, T):
        pl.semaphore_signal(barrier, inc=1, device_id={"tensor": lax.rem(me_t + i, T)},
                            device_id_type=MESH)

    slots = [slot_s[r] for r in range(S)]
    orow = iota((O, 128), 0)
    lane = iota((O, 128), 1)
    seen = jnp.zeros((O, 128), jnp.int32)
    note = jnp.zeros((O, 128), jnp.int32)
    for r in range(S):
        hit = orow == (slots[r] >> ls)
        note = jnp.where(hit & (seen == (lane & 1)), (slots[r] & (S - 1)) + 1, note)
        seen = seen + jnp.where(hit, 1, 0)
    MR = meta_out.shape[1]
    L = (iota((MR, 128), 0) - 1) * 128 + iota((MR, 128), 1) - me * (S * DRAFT)
    keyed = jnp.zeros((MR, 128), jnp.int32)
    for r in range(S):
        keyed = jnp.where((L >= DRAFT * r) & (L < DRAFT * r + DRAFT),
                          slots[r] * 4 + 1 - DRAFT * r + L, keyed)
    first = iota((MR, 128), 0) == 0
    for o in range(O):
        meta_out[o] = jnp.where(first, jnp.broadcast_to(note[o:o + 1], (MR, 128)), keyed)

    NQ, NF = S * DRAFT * GS, S * DRAFT * 2
    NC = src.shape[0]
    c = iota((1, NC), 1)
    f = c - NQ
    pre = c - NQ - NF
    is_q = c < NQ
    is_f = (c >= NQ) & (pre < 0)
    rf = jnp.zeros((1, NC), jnp.int32)
    for r in range(1, S):
        rf = rf + jnp.where(f >= r * 2 * DRAFT, 1, 0)
    rcol = jnp.where(is_q, (c >> lg) & (S - 1), jnp.where(is_f, rf, -1))
    ocol = jnp.zeros((1, NC), jnp.int32) - 1
    for r in range(S):
        ocol = jnp.where(rcol == r, slots[r] >> ls, ocol)
    rank = jnp.zeros((1, NC), jnp.int32)
    for r in range(S):
        rank = rank + jnp.where((rcol > r) & (ocol == (slots[r] >> ls)), 1, 0)
    code = (ocol * CAP + rank) * KEYS
    ckey = jnp.where(
        is_q, code + (c >> (lg + ls)) * GS + (c & (GS - 1)),
        jnp.where(is_f, code + 24 + f - rf * 2 * DRAFT,
                  (pre >> 1) * CAP * KEYS + 32 + (pre & 1)))
    OB = min(O, 8)
    jr = iota((OB * PACK, 1), 0)
    j = jr & (PACK - 1)
    jf = j - 48
    jkey = jnp.where(j < 48, (j & 1) * KEYS + (j >> 4) * GS + ((j >> 1) & (GS - 1)),
                     jnp.where(j < 60, (j & 1) * KEYS + 24 + (jf >> 2) * 2 + ((jf >> 1) & 1),
                               jnp.where(j < 62, 32 + j - 60, -1000000)))
    jkey = jkey + (jr >> 6) * CAP * KEYS
    for b in range(O // OB):
        place = jnp.where(jkey + b * OB * CAP * KEYS == ckey, 1.0, 0.0).astype(BF16)
        packed = jnp.dot(place, src[...], preferred_element_type=F32).astype(BF16)
        for k in range(K):
            pack[k, b * OB:(b + 1) * OB] = packed[:, k * HD:(k + 1) * HD].reshape(OB, PACK, HD)

    pl.semaphore_wait(barrier, O - 1 + T - 1)

    def peer(i):
        p = lax.rem(me + i, O)
        return p, {"pool": p // R, "rep": lax.rem(p, R)}

    def meta_copy(i):
        p, dev = peer(i)
        return pltpu.make_async_remote_copy(
            meta_out.at[p], meta_in.at[me], mt_send.at[p], mt_recv.at[me], dev, MESH)

    def pack_copy(k, i):
        p, dev = peer(i)
        return pltpu.make_async_remote_copy(
            pack.at[k, p], recv.at[k, me], pk_send.at[k, p], pk_recv.at[k, me], dev, MESH)

    own_copies = [pltpu.make_async_copy(meta_out.at[me], meta_in.at[me], self_sem.at[K])]
    for k in range(K):
        own_copies.append(pltpu.make_async_copy(pack.at[k, me], recv.at[k, me], self_sem.at[k]))
    for cp in own_copies:
        cp.start()
    order = list(range(1, O))
    for i in order:
        meta_copy(i).start()
    for k in range(K):
        for i in order:
            pack_copy(k, i).start()
    for k in range(K):
        pltpu.make_async_copy(
            weight.at[pl.ds(k * gw, gw), :], wbuf.at[k], w_sem.at[k]).start()

    def wait_arrival(buf, sem):
        pltpu.make_async_copy(buf, buf, sem).wait()

    own_copies[0].wait()
    for i in order:
        p, _ = peer(i)
        wait_arrival(meta_in.at[p], mt_recv.at[p])

    def row_keys():
        q = iota((NQ, 1), 0)
        qk = (((q >> lg) & (S - 1)) + 1) * KEYS + (q >> (lg + ls)) * GS + (q & (GS - 1))
        fr = iota((S * 16, 1), 0)
        e = fr & 15
        pr = iota((PR, 1), 0)
        parts = [qk]
        for kv in range(2):
            parts.append(jnp.where(e < DRAFT, ((fr >> 4) + 1) * KEYS + 24 + e * 2 + kv, -2))
            parts.append(jnp.where(pr < O, (S + 2) * KEYS + pr * 2 + kv, -2))
        return parts

    parts = row_keys()
    l128 = iota((1, 128), 1)
    jl = l128 & (PACK - 1)
    jlf = jl - 48
    stat = jnp.where(jl < 48, (jl >> 4) * GS + ((jl >> 1) & (GS - 1)),
                     24 + (jlf >> 2) * 2 + ((jlf >> 1) & 1))
    for pair in range(O // 2):
        m = jnp.where(l128 < PACK, meta_in[2 * pair, 0:1, :], meta_in[2 * pair + 1, 0:1, :])
        srcidx = 2 * pair + (l128 >> 6)
        key = jnp.where(jl < 60, m * KEYS + stat,
                        jnp.where(jl < 62, (S + 2) * KEYS + srcidx * 2 + jl - 60, -1))
        row = 0
        for part in parts:
            n = part.shape[0]
            perm[row:row + n, pair * 128:(pair + 1) * 128] = jnp.where(part == key, 1.0, 0.0).astype(BF16)
            row += n

    def out_onehots(keys):
        g = iota((O * 2 * S, 1), 0)
        hi = (g >> ls) & 1
        slot4 = (((g >> (ls + 1)) << ls) + (g & (S - 1))) * 4 + 1
        res = []
        for kk in (slot4 + hi, jnp.where(hi == 0, slot4 + 2, -1), jnp.where(hi == 1, slot4 + 2, -1)):
            res.append(jnp.transpose(jnp.where(kk == keys, 1.0, 0.0)).astype(BF16))
        return res

    total = meta_in[0]
    for o in range(1, O):
        total = total + meta_in[o]
    keep = cmat is not None
    if not keep:
        for i in order:
            meta_copy(i).wait_send()
        meta_out[0] = total

    pslot, poff = pslot_s[0], poff_s[0]
    jc = iota((1, 2 * CTX), 1)
    tc = jc >> 1
    neg = jnp.float32(-jnp.inf)
    lp = iota((1, PR + 16), 1)
    drow = iota((DRAFT * GS, PR + 16), 0) >> lg
    lane_e = iota((DRAFT * GS, PR + 16), 1)
    fresh_ok = (lane_e >= PR) & (lane_e - PR <= drow)
    scale = HD ** -0.5
    si = iota((S * GS, S * GS), 0)
    sj = iota((S * GS, S * GS), 1)
    swap = jnp.where(((si & (S - 1)) == (sj >> lg)) & ((si >> ls) == (sj & (GS - 1))), 1.0, 0.0).astype(BF16)

    def attend(k):
        took = jnp.dot(perm[...], recv[k].reshape(O * PACK, HD), preferred_element_type=F32)
        fk0 = NQ
        pk0 = fk0 + S * 16
        fv0 = pk0 + PR
        pv0 = fv0 + S * 16
        pre_k, pre_v = took[pk0:pk0 + PR].astype(BF16), took[pv0:pv0 + PR].astype(BF16)
        sc, se, xs, vs = [], [], [], []
        for s in range(S):
            q = jnp.concatenate([took[(d * S + s) * GS:(d * S + s + 1) * GS] for d in range(DRAFT)], 0).astype(BF16)
            x = kvbuf[k, s].reshape(2 * CTX, HD)
            ek = jnp.concatenate([pre_k, took[fk0 + s * 16:fk0 + s * 16 + 16].astype(BF16)], 0)
            ev = jnp.concatenate([pre_v, took[fv0 + s * 16:fv0 + s * 16 + 16].astype(BF16)], 0)
            nt = (((1,), (1,)), ((), ()))
            a = lax.dot_general(q, x, nt, preferred_element_type=F32) * scale
            b = lax.dot_general(q, ek, nt, preferred_element_type=F32) * scale
            mine = s == pslot
            lo_t = jnp.where(mine, poff, CTX)
            ok = ((jc & 1) == 0) & (tc < len_s[s]) & ((tc < lo_t) | (tc >= lo_t + O))
            pre_lim = jnp.where(mine, O, 0)
            sc.append(jnp.where(ok, a, neg))
            se.append(jnp.where(fresh_ok | (lane_e < pre_lim), b, neg))
            xs.append(x)
            vs.append(ev)
        outs = []
        for s in range(S):
            top = jnp.maximum(jnp.max(sc[s], axis=1, keepdims=True), jnp.max(se[s], axis=1, keepdims=True))
            pa, pb = jnp.exp(sc[s] - top), jnp.exp(se[s] - top)
            inv = 1.0 / (jnp.sum(pa, axis=1, keepdims=True) + jnp.sum(pb, axis=1, keepdims=True))
            wa = pltpu.roll(pa * inv, 1, 1).astype(BF16)
            wb = (pb * inv).astype(BF16)
            outs.append(jnp.dot(wa, xs[s], preferred_element_type=F32)
                        + jnp.dot(wb, vs[s], preferred_element_type=F32))
        turned = []
        for d in range(DRAFT):
            rows = jnp.concatenate([o[d * GS:(d + 1) * GS] for o in outs], 0).astype(BF16)
            turned.append(jnp.dot(swap, rows, preferred_element_type=F32))
        for g in range(GS):
            gath[k, me, :, g * HD:(g + 1) * HD] = jnp.concatenate(
                [turned[0][g * S:(g + 1) * S], turned[1][g * S:(g + 1) * S]], 0).astype(BF16)
        for g in range(half):
            gath[k, me, :, gw + g * HD:gw + (g + 1) * HD] = jnp.concatenate(
                [turned[2][g * S:(g + 1) * S], turned[2][(g + half) * S:(g + half + 1) * S]], 0).astype(BF16)

    def g_copy(k, block, way):
        dev = [{"pool": z + 1}, {"pool": z - 1}, {"rep": 1 - core}][way]
        ref = gath.at[k, block]
        return pltpu.make_async_remote_copy(ref, ref, g_send.at[k, block, way], g_recv.at[k, block], dev, MESH)

    sends = []

    def g_start(k, cond, block, way):
        sends.append((k, cond, block, way))

        @pl.when(cond)
        def _():
            g_copy(k, block, way).start()

    always = z >= 0

    def hop(k, h):
        if h == 0:
            g_start(k, z < PL - 1, me, 0)
            g_start(k, z > 0, me, 1)
            g_start(k, always, me, 2)
            return
        for way, zz in ((0, z - h), (1, z + h)):
            there = (zz >= 0) & (zz < PL)
            block = jnp.clip(zz, 0, PL - 1) * R + core

            @pl.when(there)
            def _():
                wait_arrival(gath.at[k, block], g_recv.at[k, block])

            g_start(k, there & ((z < PL - 1) if way == 0 else (z > 0)), block, way)
            g_start(k, there, block, 2)

    def other_core(k):
        for zz in range(PL):
            block = zz * R + 1 - core
            wait_arrival(gath.at[k, block], g_recv.at[k, block])

    def picked(k, mats):
        g = gath[k].reshape(O * 2 * S, gw + gw // 2)
        a = jnp.dot(mats[0], g[:, :gw], preferred_element_type=F32)
        b = jnp.dot(mats[1], g[:, gw:], preferred_element_type=F32)
        c2 = jnp.dot(mats[2], g[:, gw:], preferred_element_type=F32)
        return (a + jnp.concatenate([b, c2], 1)).astype(BF16)

    def y_copy(n, i):
        p = lax.rem(me_t + i, T)
        return pltpu.make_async_remote_copy(
            ysend.at[n, p], yrecv.at[n, me_t], y_send.at[n, p], y_recv.at[n, me_t], {"tensor": p}, MESH)

    NCH = ysend.shape[0]
    cw = N // NCH

    def share(n):
        for t in range(T):
            ysend[n, t] = ytot[t * rows_t:(t + 1) * rows_t, n * cw:(n + 1) * cw].astype(BF16)
        for i in range(1, T):
            y_copy(n, i).start()

    def project(k):
        pltpu.make_async_copy(weight.at[pl.ds(k * gw, gw), :], wbuf.at[k], w_sem.at[k]).wait()
        if keep:
            rows = picked(k, [cmat[x] for x in range(3)])
            for n in range(NCH):
                cols = slice(n * cw, (n + 1) * cw)
                y = jnp.dot(rows, wbuf[k, :, cols], preferred_element_type=F32)
                ytot[:, cols] = y if k == 0 else ytot[:, cols] + y
                if k == K - 1:
                    share(n)
        else:
            def body(t, carry):
                rows = picked(k, out_onehots(meta_out[0, pl.ds(1 + t, 1), :]))
                at = pl.ds(pl.multiple_of(t * 128, 128), 128)
                y = jnp.dot(rows, wbuf[k], preferred_element_type=F32)
                ytot[at, :] = y if k == 0 else ytot[at, :] + y
                return carry

            lax.fori_loop(0, NT, body, 0)
            if k == K - 1:
                for n in range(NCH):
                    share(n)

    for step in range(K + PL):
        if step < K:
            k = step
            pltpu.make_async_copy(cache.at[:, :, :, pl.ds(k * HD, HD)], kvbuf.at[k], kv_sem.at[k]).wait()
            own_copies[1 + k].wait()
            for i in order:
                p, _ = peer(i)
                wait_arrival(recv.at[k, p], pk_recv.at[k, p])
            attend(k)
            hop(k, 0)
            if keep and k == 0:
                for t in range(NT):
                    for x, m in enumerate(out_onehots(total[1 + t:2 + t])):
                        cmat[x, t * 128:(t + 1) * 128, :] = m
        for h in range(PL - 1, 0, -1):
            if 0 <= step - h < K:
                hop(step - h, h)
        k = step - PL
        if 0 <= k < K:
            other_core(k)
            project(k)

    for n in range(NCH):
        cols = slice(n * cw, (n + 1) * cw)
        y = ytot[pl.ds(pl.multiple_of(me_t * rows_t, 32), rows_t), cols]
        for i in range(1, T):
            p = lax.rem(me_t + i, T)
            wait_arrival(yrecv.at[n, p], y_recv.at[n, p])
            y = y + yrecv[n, p].astype(F32)
        out[:, cols] = y.astype(BF16)

    if keep:
        for i in order:
            meta_copy(i).wait_send()
    for k in range(K):
        for i in order:
            pack_copy(k, i).wait_send()
    for k, cond, block, way in sends:
        @pl.when(cond)
        def _():
            g_copy(k, block, way).wait_send()
    for n in range(NCH):
        for i in range(1, T):
            y_copy(n, i).wait_send()


def on_device(request_slot, lengths, prefill_slot, prefill_offset, queries, new_kv, kv_cache,
              prefill_kv, out_weight):
    PLn, R, T = lax.axis_size("pool"), lax.axis_size("rep"), lax.axis_size("tensor")
    O = PLn * R
    S = lengths.shape[0]
    CTX = kv_cache.shape[1]
    K = kv_cache.shape[3] // HD
    GS = queries.shape[2] // kv_cache.shape[3]
    N = out_weight.shape[1]
    rows = O * S * DRAFT
    NT = up(rows, 128) // 128
    gw = GS * HD
    src_q = queries.reshape(S, DRAFT, K, GS, HD).transpose(1, 0, 3, 2, 4).reshape(-1, K * HD)
    src_f = new_kv.reshape(-1, K * HD)
    src_p = prefill_kv.reshape(-1, K * HD)
    src = jnp.concatenate([src_q, src_f, src_p], 0)
    PR = max(16, O)
    MR = up(1 + NT, 8)
    perm_rows = S * DRAFT * GS + 2 * (S * 16 + PR)
    keep = NT <= 2
    NCH = 2
    dims = (S, O, R, T, K, CTX, GS, N, NT)
    scratch = [
        pltpu.VMEM((K, S, CTX, 2, HD), BF16),
        pltpu.VMEM((K, gw, N), BF16),
        pltpu.VMEM((K, O, PACK, HD), BF16),
        pltpu.VMEM((K, O, PACK, HD), BF16),
        pltpu.VMEM((O, MR, 128), jnp.int32),
        pltpu.VMEM((O, MR, 128), jnp.int32),
        pltpu.VMEM((perm_rows, O * PACK), BF16),
    ]
    if keep:
        scratch.append(pltpu.VMEM((3, NT * 128, O * 2 * S), BF16))
    scratch += [
        pltpu.VMEM((K, O, 2 * S, gw + gw // 2), BF16),
        pltpu.VMEM((NT * 128, N), F32),
        pltpu.VMEM((NCH, T, rows // T, N // NCH), BF16),
        pltpu.VMEM((NCH, T, rows // T, N // NCH), BF16),
    ]
    D = pltpu.SemaphoreType.DMA
    scratch += [D((K,)), D((K,)), D((K + 1,)), D((K, O)), D((K, O)), D((O,)), D((O,)),
                D((K, O, 3)), D((K, O)), D((NCH, T)), D((NCH, T))]
    if keep:
        body = functools.partial(kernel, dims)
    else:
        def body(*refs):
            return kernel(dims, *refs[:15], None, *refs[15:])
    smem = pl.BlockSpec(memory_space=pltpu.SMEM)
    vmem = pl.BlockSpec(memory_space=pltpu.VMEM)
    hbm = pl.BlockSpec(memory_space=pl.ANY)
    return pl.pallas_call(
        body,
        out_shape=jax.ShapeDtypeStruct((rows // T, N), BF16),
        in_specs=[smem] * 4 + [vmem, hbm, hbm],
        out_specs=vmem,
        scratch_shapes=scratch,
        compiler_params=pltpu.CompilerParams(
            collective_id=0, has_side_effects=True, vmem_limit_bytes=56 * 1024 * 1024),
        cost_estimate=pl.CostEstimate(flops=4 * 10 ** 9, bytes_accessed=12 * 10 ** 6, transcendentals=10 ** 6),
    )(request_slot, lengths, prefill_slot, prefill_offset, src, kv_cache, out_weight)


def solution(mesh):
    owner = ("groups", "pool", "rep")
    return jax.shard_map(
        on_device,
        mesh=mesh,
        in_specs=(
            P(owner), P(owner), P(owner), P(owner),
            P(owner, None, "tensor"),
            P(owner, None, None, "tensor"),
            P(owner, None, None, "tensor"),
            P("groups", ("pool", "rep"), None, "tensor"),
            P("tensor", ("pool", "rep")),
        ),
        out_specs=P(("groups", "tensor"), ("pool", "rep")),
        check_vma=False,
    )
```
